256 devices in a mesh: chan: 32 (over z, x_hi, core), band: 8 (over y, x_lo).
Axes of the slice: x: 4 (x_hi: 2, x_lo: 2; x = x_hi * 2 + x_lo), y: 4, z: 8, core: 2. Of those that a mesh axis runs over, the one named last changes fastest.
Arguments:
- spectra: bfloat16 [1024, 128, 1152], P('chan', 'band'), parts along dimension 1, may hold values from -6 to 6
- weights: float32 [128, 1152], P('band'), parts along dimension 0, may hold values from 0.1 to 10
Outputs:
- cross_power: bfloat16 [128, 1024, 1024], P('band', 'chan'), parts along dimension 0
The draws below stay inside these ranges and needn't reach their ends.
There are 8 independent parts, one for each index of `band`. The reference program is written for one: setup_inputs(seed, part) draws one part's arguments, and reference() takes and returns one part's arrays. A program takes and returns all parts, laid end to end along the dimension named above; each array names one. Nothing has to cross between parts.
All inputs are finite; a program needn't handle non-finite values.
Results may differ from the reference program's by a relative error of at most 0.009.
Values may be sent and summed in bfloat16 or wider, within the bound.
A program may use at most 128 MiB of HBM per device.

```python
import math
import jax
import jax.numpy as jnp
from jax import lax

L = 16
M_L = 1152
CH_TOT = 1024


def block_scale(rng, extent, split, least, top_value):
    gain = 1.0
    for position, shards_of in split:
        heights = jax.random.uniform(jax.random.fold_in(jax.random.fold_in(rng, 6), position), (shards_of,), jnp.float32, least / len(split), top_value / len(split))
        gain = gain * jnp.repeat(jnp.exp(heights), extent[position] // shards_of).reshape((-1,) + (1,) * (len(extent) - 1 - position))
    return gain


def noise(rng, dims, scale, limit, shards=(), dtype=jnp.bfloat16):
    drawn = scale * jax.random.normal(rng, dims, jnp.float32)
    if shards:
        drawn = drawn * block_scale(rng, dims, shards, -0.22, 0.18)
    return jnp.clip(drawn, -limit, limit).astype(dtype)


def setup_inputs(seed: int = 0, part: int = 0) -> dict:
    key_list = jax.random.split(jax.random.key(seed), 3)
    part_keys = jax.random.split(jax.random.fold_in(key_list[2], part), 3)
    return {
        "spectra": noise(part_keys[0], (CH_TOT, L, M_L), 1.0, 6.0, ((0, 32),)),
        "weights": jnp.clip(jnp.exp(jax.random.uniform(part_keys[1], (L, M_L), jnp.float32, math.log(0.1), math.log(10.0))), 0.1, 10.0),
    }


def reference(spectra, weights):
    weight_sum = jnp.sum(weights, axis=1)
    scaled = weights / weight_sum[:, None]
    weighted = (spectra.astype(jnp.float32) * scaled[None, :, :]).astype(jnp.bfloat16)

    def one_multipole(pair):
        left, right = pair
        return jnp.dot(left, right.T, preferred_element_type=jnp.float32).astype(jnp.bfloat16)

    return lax.map(one_multipole, (jnp.transpose(weighted, (1, 0, 2)), jnp.transpose(spectra, (1, 0, 2))))
```

```python
import functools

import jax
import jax.numpy as jnp
from jax import lax
from jax.experimental import pallas as pl
from jax.experimental.pallas import tpu as pltpu
from jax.sharding import PartitionSpec as P

MESH = pl.DeviceIdType.MESH
BF16 = jnp.bfloat16
F32 = jnp.float32

ZS = 8
OWN = 32
BANDL = 16
ML = 1152
CH = 1024


def step_of(t):
    u, dc = t // 2, t % 2
    mag = 4 - (u + 1) // 2
    return jnp.where(u % 2 == 1, mag, 8 - mag) % 8, dc


def kernel(
    x_ref, w_ref, o_ref, send, full, left, stage, s1, r1, s2, r2, s3, r3, own_sem
):
    k = lax.axis_index("chan")
    core, xh, z = k % 2, (k // 2) % 2, k // 4
    me = 2 * z + core

    def chan(zz, xx, cc):
        return (zz * 2 + xx) * 2 + cc

    def to(t):
        dz, dc = step_of(t)
        return (z + dz) % 8, (core + dc) % 2

    def source(t):
        dz, dc = step_of(t)
        return (z + 8 - dz) % 8, (core + dc) % 2

    partner = chan(z, 1 - xh, core)
    barrier = pltpu.get_barrier_semaphore()

    def greet(t, carry):
        zz, cc = source(t)
        pl.semaphore_signal(
            barrier, inc=1, device_id={"chan": chan(zz, xh, cc)}, device_id_type=MESH
        )
        return carry

    lax.fori_loop(0, 14, greet, 0)
    greet(15, 0)
    pl.semaphore_signal(barrier, inc=1, device_id={"chan": partner}, device_id_type=MESH)

    for j in range(ML // 128):
        cols = pl.ds(j * 128, 128)
        send[:, :, cols] = jnp.swapaxes(x_ref[:, :, cols], 0, 1)

    pl.semaphore_wait(barrier, 16)

    def rows(kk):
        return pl.ds(pl.multiple_of(kk * OWN, OWN), OWN)

    def first(t):
        zz, cc = to(t)
        return pltpu.make_async_remote_copy(
            src_ref=send.at[2 * zz + cc],
            dst_ref=full.at[rows(k)],
            send_sem=s1.at[t],
            recv_sem=r1.at[t],
            device_id={"chan": chan(zz, xh, cc)},
            device_id_type=MESH,
        )

    def across(t):
        zz, cc = source(t)
        block = full.at[rows(chan(zz, xh, cc))]
        return pltpu.make_async_remote_copy(
            src_ref=block,
            dst_ref=block,
            send_sem=s2.at[t],
            recv_sem=r2.at[t],
            device_id={"chan": partner},
            device_id_type=MESH,
        )

    def start_first(t, carry):
        first(t).start()
        return carry

    lax.fori_loop(0, 14, start_first, 0)
    start_first(15, 0)
    full[rows(k), :] = send[me]
    across(14).start()

    def forward(t, carry):
        first(t).wait_recv()
        across(t).start()
        return carry

    lax.fori_loop(0, 14, forward, 0)
    forward(15, 0)

    weight = w_ref[pl.ds(me, 1), :]
    scaled = weight / jnp.sum(weight, axis=1, keepdims=True)

    def arrived(t, carry):
        across(t).wait_recv()
        return carry

    lax.fori_loop(0, 16, arrived, 0)

    def back(t):
        zz, cc = to(t)
        return pltpu.make_async_remote_copy(
            src_ref=stage.at[t],
            dst_ref=o_ref.at[me],
            send_sem=s3.at[t],
            recv_sem=r3.at[t],
            device_id={"chan": chan(zz, xh, cc)},
            device_id_type=MESH,
        )

    def chunk(u, last):
        for a in range(4):
            zz, cc = to(4 * u + a)
            block = full[rows(chan(zz, xh, cc)), :].astype(F32)
            left[pl.ds(a * OWN, OWN), :] = (block * scaled).astype(BF16)
        for n in range(CH // 256):
            tile = lax.dot_general(
                left[...],
                full[pl.ds(n * 256, 256), :],
                (((1,), (1,)), ((), ())),
                preferred_element_type=F32,
            ).astype(BF16)
            for a in range(4):
                stage[4 * u + a, :, pl.ds(n * 256, 256)] = tile[a * OWN : (a + 1) * OWN]
        for a in range(4):
            if not (last and a == 2):
                back(4 * u + a).start()

    def chunk_step(u, carry):
        chunk(u, False)
        return carry

    lax.fori_loop(0, 3, chunk_step, 0)
    chunk(3, True)
    own = pltpu.make_async_copy(stage.at[14], o_ref.at[me], own_sem)
    own.start()

    def finish(t, carry):
        first(t).wait_send()
        back(t).wait()
        return carry

    lax.fori_loop(0, 14, finish, 0)
    finish(15, 0)

    def sent(t, carry):
        across(t).wait_send()
        return carry

    lax.fori_loop(0, 16, sent, 0)
    own.wait()


def per_device(spectra, weights):
    return pl.pallas_call(
        kernel,
        out_shape=jax.ShapeDtypeStruct((BANDL, OWN, CH), BF16),
        in_specs=[pl.BlockSpec(memory_space=pltpu.VMEM)] * 2,
        out_specs=pl.BlockSpec(memory_space=pl.ANY),
        scratch_shapes=[
            pltpu.VMEM((BANDL, OWN, ML), BF16),
            pltpu.VMEM((CH, ML), BF16),
            pltpu.VMEM((4 * OWN, ML), BF16),
            pltpu.VMEM((BANDL, OWN, CH), BF16),
        ]
        + [pltpu.SemaphoreType.DMA((16,))] * 6
        + [pltpu.SemaphoreType.DMA],
        compiler_params=pltpu.CompilerParams(
            collective_id=0, has_side_effects=True, vmem_limit_bytes=32 << 20
        ),
        cost_estimate=pl.CostEstimate(
            flops=2 * BANDL * OWN * CH * ML, bytes_accessed=4 << 20, transcendentals=0
        ),
        name="cross",
    )(spectra, weights)


def solution(mesh):
    placed = (P("chan", "band", None), P("band", None))
    return jax.shard_map(
        per_device, mesh=mesh, in_specs=placed, out_specs=P("band", "chan", None), check_vma=False
    )
```

```python
import functools

import jax
import jax.numpy as jnp
from jax import lax
from jax.experimental import pallas as pl
from jax.experimental.pallas import tpu as pltpu
from jax.sharding import PartitionSpec as P

MESH = pl.DeviceIdType.MESH
BF16 = jnp.bfloat16
F32 = jnp.float32

ZS = 8
OWN = 32
BANDL = 16
ML = 1152
CH = 1024


def step_of(t):
    u, dx = t // 2, t % 2
    mag = 4 - (u + 1) // 2
    return jnp.where(u % 2 == 1, mag, 8 - mag) % 8, dx


def kernel(
    x_ref, w_ref, o_ref, send, full, left, stage, s1, r1, s2, r2, s3, r3, own_sem
):
    k = lax.axis_index("chan")
    core, xh, z = k % 2, (k // 2) % 2, k // 4
    me = 2 * z + xh

    def chan(zz, xx, cc):
        return (zz * 2 + xx) * 2 + cc

    def to(t):
        dz, dx = step_of(t)
        return (z + dz) % 8, (xh + dx) % 2

    def source(t):
        dz, dx = step_of(t)
        return (z + 8 - dz) % 8, (xh + dx) % 2

    partner = chan(z, xh, 1 - core)
    barrier = pltpu.get_barrier_semaphore()

    def greet(t, carry):
        zz, xx = source(t)
        pl.semaphore_signal(
            barrier, inc=1, device_id={"chan": chan(zz, xx, core)}, device_id_type=MESH
        )
        return carry

    lax.fori_loop(0, 14, greet, 0)
    greet(15, 0)
    pl.semaphore_signal(barrier, inc=1, device_id={"chan": partner}, device_id_type=MESH)

    for j in range(ML // 128):
        cols = pl.ds(j * 128, 128)
        send[:, :, cols] = jnp.swapaxes(x_ref[:, :, cols], 0, 1)

    pl.semaphore_wait(barrier, 16)

    def rows(kk):
        return pl.ds(pl.multiple_of(kk * OWN, OWN), OWN)

    def first(t):
        zz, xx = to(t)
        return pltpu.make_async_remote_copy(
            src_ref=send.at[2 * zz + xx],
            dst_ref=full.at[rows(k)],
            send_sem=s1.at[t],
            recv_sem=r1.at[t],
            device_id={"chan": chan(zz, xx, core)},
            device_id_type=MESH,
        )

    def across(t):
        zz, xx = source(t)
        block = full.at[rows(chan(zz, xx, core))]
        return pltpu.make_async_remote_copy(
            src_ref=block,
            dst_ref=block,
            send_sem=s2.at[t],
            recv_sem=r2.at[t],
            device_id={"chan": partner},
            device_id_type=MESH,
        )

    def start_first(t, carry):
        first(t).start()
        return carry

    lax.fori_loop(0, 14, start_first, 0)
    start_first(15, 0)
    full[rows(k), :] = send[me]
    across(14).start()

    def forward(t, carry):
        first(t).wait_recv()
        across(t).start()
        return carry

    lax.fori_loop(0, 14, forward, 0)
    forward(15, 0)

    weight = w_ref[pl.ds(me, 1), :]
    scaled = weight / jnp.sum(weight, axis=1, keepdims=True)

    def arrived(t, carry):
        across(t).wait_recv()
        return carry

    lax.fori_loop(0, 16, arrived, 0)

    def back(t):
        zz, xx = to(t)
        return pltpu.make_async_remote_copy(
            src_ref=stage.at[t],
            dst_ref=o_ref.at[me],
            send_sem=s3.at[t],
            recv_sem=r3.at[t],
            device_id={"chan": chan(zz, xx, core)},
            device_id_type=MESH,
        )

    def chunk(u, last):
        for a in range(4):
            zz, xx = to(4 * u + a)
            block = full[rows(chan(zz, xx, core)), :].astype(F32)
            left[pl.ds(a * OWN, OWN), :] = (block * scaled).astype(BF16)
        for n in range(CH // 256):
            tile = lax.dot_general(
                left[...],
                full[pl.ds(n * 256, 256), :],
                (((1,), (1,)), ((), ())),
                preferred_element_type=F32,
            ).astype(BF16)
            for a in range(4):
                stage[4 * u + a, :, pl.ds(n * 256, 256)] = tile[a * OWN : (a + 1) * OWN]
        for a in range(4):
            if not (last and a == 2):
                back(4 * u + a).start()

    def chunk_step(u, carry):
        chunk(u, False)
        return carry

    lax.fori_loop(0, 3, chunk_step, 0)
    chunk(3, True)
    own = pltpu.make_async_copy(stage.at[14], o_ref.at[me], own_sem)
    own.start()

    def finish(t, carry):
        first(t).wait_send()
        back(t).wait()
        return carry

    lax.fori_loop(0, 14, finish, 0)
    finish(15, 0)

    def sent(t, carry):
        across(t).wait_send()
        return carry

    lax.fori_loop(0, 16, sent, 0)
    own.wait()


def per_device(spectra, weights):
    return pl.pallas_call(
        kernel,
        out_shape=jax.ShapeDtypeStruct((BANDL, OWN, CH), BF16),
        in_specs=[pl.BlockSpec(memory_space=pltpu.VMEM)] * 2,
        out_specs=pl.BlockSpec(memory_space=pl.ANY),
        scratch_shapes=[
            pltpu.VMEM((BANDL, OWN, ML), BF16),
            pltpu.VMEM((CH, ML), BF16),
            pltpu.VMEM((4 * OWN, ML), BF16),
            pltpu.VMEM((BANDL, OWN, CH), BF16),
        ]
        + [pltpu.SemaphoreType.DMA((16,))] * 6
        + [pltpu.SemaphoreType.DMA],
        compiler_params=pltpu.CompilerParams(
            collective_id=0, has_side_effects=True, vmem_limit_bytes=32 << 20
        ),
        cost_estimate=pl.CostEstimate(
            flops=2 * BANDL * OWN * CH * ML, bytes_accessed=4 << 20, transcendentals=0
        ),
        name="cross",
    )(spectra, weights)


def solution(mesh):
    placed = (P("chan", "band", None), P("band", None))
    return jax.shard_map(
        per_device, mesh=mesh, in_specs=placed, out_specs=P("band", "chan", None), check_vma=False
    )
```

```python
import jax
import jax.numpy as jnp
from jax import lax
from jax.experimental import pallas as pl
from jax.experimental.pallas import tpu as pltpu
from jax.sharding import PartitionSpec as P

MESH = pl.DeviceIdType.MESH
BF16 = jnp.bfloat16
F32 = jnp.float32

ZS = 8
OWN = 32
BANDL = 16
ML = 1152
CH = 1024


def kernel(
    x_hbm, w_hbm, o_ref, x_ref, w_ref, send, own, zb, wown, wz, stage,
    in_sem, x_send, x_recv, c_send, co_recv, cz_recv, z_send, z_recv, o_send, o_recv,
):
    loads = [
        pltpu.make_async_copy(x_hbm, x_ref, in_sem.at[0]),
        pltpu.make_async_copy(w_hbm, w_ref, in_sem.at[1]),
    ]
    for load in loads:
        load.start()
    dev = lax.axis_index("chan")
    core, xh, z = dev % 2, (dev // 2) % 2, dev // 4

    def chan(zz, xx, cc):
        return {"chan": ((zz % ZS) * 2 + xx) * 2 + cc}

    def up(way, k):
        return (z + ZS + jnp.where(way == 0, k, -k)) % ZS

    barrier = pltpu.get_barrier_semaphore()

    def greet(t, carry):
        pl.semaphore_signal(
            barrier, inc=1, device_id=chan(z + t // 2, (xh + t) % 2, core), device_id_type=MESH
        )
        return carry

    lax.fori_loop(1, 16, greet, 0)
    pl.semaphore_signal(barrier, inc=1, device_id=chan(z, xh, 1 - core), device_id_type=MESH)

    def part(cc, hh):
        return pl.ds(pl.multiple_of((cc * 2 + hh) * OWN, OWN), OWN)

    def remote(src, dst, s, r, to):
        return pltpu.make_async_remote_copy(
            src_ref=src, dst_ref=dst, send_sem=s, recv_sem=r, device_id=to, device_id_type=MESH
        )

    def active(way, k, j):
        return jnp.logical_or(j + k < 4, (z + k + way) % 2 == 0)

    loads[0].wait()
    for c in range(ML // 128):
        cols = pl.ds(c * 128, 128)
        send[:, :, cols] = jnp.swapaxes(x_ref[:, :, cols], 0, 1)
    pl.semaphore_wait(barrier, 16)

    def z_own(way, k, hh, src):
        remote(
            src, zb.at[way, k - 1, 0, part(core, hh)], z_send, z_recv.at[way, k - 1, 0, hh],
            chan(up(way, 1), xh, core),
        ).start()

    def x_copy(p):
        return remote(
            send.at[2 * p + 1 - xh], own.at[p, part(core, xh)], x_send, x_recv.at[p],
            chan(z, 1 - xh, core),
        )

    def x_wait(p):
        block = own.at[p, part(core, 1 - xh)]
        remote(block, block, x_send, x_recv.at[p], chan(z, 1 - xh, core)).wait_recv()

    def c_own(p, hh, src):
        remote(
            src, own.at[p, part(core, hh)], c_send, co_recv.at[p, hh], chan(z, xh, 1 - core)
        ).start()

    def out(k):
        for way in range(2):
            p = up(way, k)
            src = send.at[2 * p + xh]
            if k == 4:
                pl.when(active(way, 4, 0))(lambda: z_own(way, 4, xh, src))
                if way == 0:
                    x_copy(p).start()
            else:
                z_own(way, k, xh, src)
                x_copy(p).start()

    for k in (4, 3, 2, 1):
        out(k)
    x_copy(z).start()

    def keep(p, carry):
        block = send.at[2 * p + xh]
        c_own(p, xh, block)
        own[p, part(core, xh), :] = block[...]
        return carry

    lax.fori_loop(0, ZS, keep, 0)

    def take_x(way, k):
        p = up(way, k)
        x_wait(p)
        src = own.at[p, part(core, 1 - xh)]
        if k == 4:
            for w in range(2):
                pl.when(active(w, 4, 0))(lambda: z_own(w, 4, 1 - xh, src))
        elif k > 0:
            z_own(way, k, 1 - xh, src)
        c_own(p, 1 - xh, src)

    def take_z(way, k, j, hh):
        def go():
            block = zb.at[way, k, j - 1, part(core, hh)]
            remote(
                block, block, z_send, z_recv.at[way, k, j - 1, hh], chan(z, xh, core)
            ).wait_recv()
            if k > 0:
                remote(
                    block, zb.at[way, k - 1, j, part(core, hh)], z_send,
                    z_recv.at[way, k - 1, j, hh], chan(up(way, 1), xh, core),
                ).start()
            remote(
                block, block, c_send, cz_recv.at[way, k, j - 1, hh], chan(z, xh, 1 - core)
            ).start()

        if j + k == 4:
            pl.when(active(way, k, j))(go)
        else:
            go()

    def both(k, j, hh):
        take_z(0, k, j, hh)
        take_z(1, k, j, hh)

    def scaled(p):
        return w_ref[pl.ds(2 * p + xh, 1), :]

    def mine():
        return pl.ds(pl.multiple_of(core * 2 * OWN, 2 * OWN), 2 * OWN)

    def natural(ref):
        return jnp.concatenate([ref[i * OWN : (i + 1) * OWN, :] for i in (0, 2, 1, 3)], axis=0)

    def dot(left, right):
        return lax.dot_general(
            left, right, (((1,), (1,)), ((), ())), preferred_element_type=F32
        ).astype(BF16)

    def emit(slot, value, p, row_z, col_z, home):
        stage[slot, 0] = value[:OWN]
        stage[slot, 1] = value[OWN:]
        place = o_ref.at[2 * p + xh, :, pl.ds(pl.multiple_of(col_z * 128, 128), 128)]
        if home:
            pltpu.make_async_copy(stage.at[slot, xh], place, o_recv).start()
            halves = (1 - xh,)
        else:
            halves = (0, 1)
        for hh in halves:
            remote(stage.at[slot, hh], place, o_send, o_recv, chan(row_z, hh, core)).start()

    def weigh(block, p):
        return (block.astype(F32) * scaled(p)).astype(BF16)

    def pair(way, k, j):
        p, far = up(way, k), up(way, -j)
        for hh in range(2):
            block = zb.at[way, k, j - 1, part(1 - core, hh)]
            remote(
                block, block, c_send, cz_recv.at[way, k, j - 1, hh], chan(z, xh, 1 - core)
            ).wait_recv()
        block = zb.at[way, k, j - 1]
        slot = 2 * ((way * 4 + k) * 4 + j - 1)
        theirs = weigh(zb[way, k, j - 1, mine(), :], p)

        @pl.when(k == 0)
        def _():
            wz[way, j - 1] = theirs

        emit(slot, dot(theirs, natural(own.at[p])), p, far, z, False)
        emit(slot + 1, dot(wown[p], natural(block)), p, z, far, True)

    def pairs(j):
        def step(t, carry):
            way, k = t % 2, (4 - j) - t // 2
            pl.when(active(way, k, j))(lambda: pair(way, k, j))
            return carry

        lax.fori_loop(0, 2 * (5 - j), step, 0)

    def cross(way, ja, jb):
        value = dot(wz[way, ja - 1], natural(zb.at[1 - way, 0, jb - 1]))
        slot = 72 + (way * 4 + ja - 1) * 4 + jb - 1
        emit(slot, value, z, up(way, -ja), up(way, jb), False)

    def crosses(j):
        def step(t, carry):
            way, i = t % 2, t // 2
            far = i < j
            cross(way, jnp.where(far, j, i - j + 1), jnp.where(far, i + 1, j))
            return carry

        lax.fori_loop(0, 2 * (2 * j - 1), step, 0)

    def crosses_last():
        way = z % 2

        def step(t, carry):
            i = t // 2
            far = t % 2 == 0
            cross(
                jnp.where(far, way, 1 - way), jnp.where(far, 4, i + 1), jnp.where(far, i + 1, 4)
            )
            return carry

        lax.fori_loop(0, 6, step, 0)

    def diagonal(p, carry):
        for hh in range(2):
            block = own.at[p, part(1 - core, hh)]
            remote(
                block, block, c_send, co_recv.at[p, hh], chan(z, xh, 1 - core)
            ).wait_recv()
        left = weigh(own[p, mine(), :], p)
        wown[p] = left
        emit(64 + p, dot(left, natural(own.at[p])), p, z, z, True)
        return carry

    take_x(0, 4)
    both(3, 1, xh)
    take_x(0, 3)
    both(2, 1, xh)
    take_x(1, 3)
    both(1, 1, xh)
    take_x(0, 2)
    both(0, 1, xh)
    take_x(1, 2)
    both(3, 1, 1 - xh)
    take_x(0, 1)
    both(2, 1, 1 - xh)
    take_x(1, 1)
    both(1, 1, 1 - xh)
    take_x(0, 0)
    loads[1].wait()
    weights = w_ref[...]
    w_ref[...] = weights / jnp.sum(weights, axis=1, keepdims=True)
    lax.fori_loop(0, ZS, diagonal, 0)
    both(0, 1, 1 - xh)
    pairs(1)
    for j in (2, 3, 4):
        for hh in (xh, 1 - xh):
            for k in range(4 - j, -1, -1):
                both(k, j, hh)
        crosses(j - 1)
        pairs(j)
    crosses_last()

    def drain(ref, sem):
        pltpu.make_async_copy(ref, ref, sem).wait()

    drain(o_ref, o_recv)
    drain(stage.at[pl.ds(0, 52)], o_send)
    drain(own, z_send)
    drain(zb.at[0, pl.ds(0, 3)], c_send)
    drain(send.at[pl.ds(0, 8)], x_send)


def per_device(spectra, weights):
    dma = pltpu.SemaphoreType.DMA
    return pl.pallas_call(
        kernel,
        out_shape=jax.ShapeDtypeStruct((BANDL, OWN, CH), BF16),
        in_specs=[pl.BlockSpec(memory_space=pl.ANY)] * 2,
        out_specs=pl.BlockSpec(memory_space=pl.ANY),
        scratch_shapes=[
            pltpu.VMEM((OWN, BANDL, ML), BF16),
            pltpu.VMEM((BANDL, ML), F32),
            pltpu.VMEM((BANDL, OWN, ML), BF16),
            pltpu.VMEM((ZS, 4 * OWN, ML), BF16),
            pltpu.VMEM((2, 4, 4, 4 * OWN, ML), BF16),
            pltpu.VMEM((ZS, 2 * OWN, ML), BF16),
            pltpu.VMEM((2, 4, 2 * OWN, ML), BF16),
            pltpu.VMEM((104, 2, OWN, 128), BF16),
            dma((2,)),
            dma,
            dma((ZS,)),
            dma,
            dma((ZS, 2)),
            dma((2, 4, 4, 2)),
            dma,
            dma((2, 4, 4, 2)),
            dma,
            dma,
        ],
        compiler_params=pltpu.CompilerParams(
            collective_id=0, has_side_effects=True, vmem_limit_bytes=60 << 20
        ),
        cost_estimate=pl.CostEstimate(
            flops=2 * BANDL * OWN * CH * ML, bytes_accessed=4 << 20, transcendentals=0
        ),
        name="cross",
    )(spectra, weights)


def solution(mesh):
    placed = (P("chan", "band", None), P("band", None))
    return jax.shard_map(
        per_device, mesh=mesh, in_specs=placed, out_specs=P("band", "chan", None), check_vma=False
    )
```

```python
import jax
import jax.numpy as jnp
from jax import lax
from jax.experimental import pallas as pl
from jax.experimental.pallas import tpu as pltpu
from jax.sharding import PartitionSpec as P

MESH = pl.DeviceIdType.MESH
BF16 = jnp.bfloat16
F32 = jnp.float32

ZS = 8
OWN = 32
PER = 128
BANDL = 16
ML = 1152
CH = 1024

ORDER = (((0, 4), (0, 2), (1, 2), (0, 0)), ((0, 3), (1, 3), (0, 1), (1, 1)))


PLAN = (
    (
        ('F', 0, 4),
        ('F', 1, 2),
        ('F', 0, 2),
        ('F', 0, 0),
        ('O', 0, 4),
        ('T', 1, 2, 1, 0),
        ('T', 0, 2, 1, 0),
        ('O', 0, 2),
        ('O', 1, 2),
        ('T', 1, 2, 1, 1),
        ('T', 0, 2, 1, 1),
        ('B', 0, 2, 1),
        ('B', 1, 2, 1),
        ('O', 0, 0),
        ('T', 0, 2, 2, 0),
        ('T', 0, 2, 2, 1),
        ('T', 0, 0, 1, 0),
        ('T', 0, 0, 1, 1),
        ('T', 1, 0, 1, 0),
        ('T', 1, 0, 1, 1),
        ('W', 0, 7, 1),
        ('X', 7, 1, 0, 2),
        ('X', 1, 1, 0, 1),
        ('B', 0, 2, 2),
        ('T', 0, 0, 2, 0),
        ('T', 0, 0, 2, 1),
        ('T', 1, 0, 2, 0),
        ('T', 1, 0, 2, 1),
        ('W', 6, 2),
        ('X', 6, 1, 0, 3),
        ('X', 2, 1, 0, 1),
        ('X', 1, 2, 6, 2),
        ('T', 0, 0, 3, 0),
        ('T', 0, 0, 3, 1),
        ('T', 1, 0, 3, 0),
        ('T', 1, 0, 3, 1),
        ('W', 5, 3),
        ('X', 5, 1, 0, 4),
        ('X', 7, 1, 2, 2),
        ('X', 3, 1, 6, 2),
        ('X', 6, 1, 3, 1),
        ('X', 3, 1, 0, 1),
        ('H', 0, 4, 4, 1),
        ('H', 0, 2, 4, 3),
        ('H', 1, 2, 2, 2),
        ('T', 0, 0, 4, 0),
        ('T', 0, 0, 4, 1),
        ('W', 4),
        ('X', 4, 1, 0, 4),
        ('X', 1, 3, 4, 2),
        ('H', 0, 0, 0, 4),
        ('H', 0, 0, 4, 4),
    ),
    (
        ('F', 0, 3),
        ('F', 1, 3),
        ('O', 0, 3),
        ('T', 0, 3, 1, 0),
        ('F', 0, 1),
        ('F', 1, 1),
        ('O', 1, 3),
        ('T', 0, 3, 1, 1),
        ('T', 0, 1, 1, 0),
        ('T', 1, 1, 1, 0),
        ('T', 0, 1, 1, 1),
        ('T', 1, 1, 1, 1),
        ('O', 0, 1),
        ('O', 1, 1),
        ('B', 0, 1, 1),
        ('B', 1, 1, 1),
        ('B', 0, 3, 1),
        ('T', 0, 1, 2, 0),
        ('T', 1, 1, 2, 0),
        ('T', 0, 1, 2, 1),
        ('T', 1, 1, 2, 1),
        ('B', 0, 1, 2),
        ('B', 1, 1, 2),
        ('T', 0, 1, 3, 0),
        ('T', 0, 1, 3, 1),
        ('B', 0, 1, 3),
        ('H', 1, 3, 3, 1),
        ('H', 0, 3, 4, 2),
        ('H', 1, 1, 1, 3),
        ('H', 0, 1, 4, 4),
    ),
)


def place(way, k):
    return k if way else (ZS - k) % ZS


def kernel(
    x_hbm, w_hbm, o_ref, x_ref, w_ref, send, ring, weighted, stage, found,
    in_sem, l_send, l_recv, z_send, z_recv, o_send, o_recv,
):
    loads = [
        pltpu.make_async_copy(x_hbm, x_ref, in_sem.at[0]),
        pltpu.make_async_copy(w_hbm, w_ref, in_sem.at[1]),
    ]
    for load in loads:
        load.start()
    dev = lax.axis_index("chan")
    core, xh, z = dev % 2, (dev // 2) % 2, dev // 4

    def chan(zz, xx, cc):
        return {"chan": ((zz % ZS) * 2 + xx) * 2 + cc}

    barrier = pltpu.get_barrier_semaphore()
    for there in (
        chan(z + 1, xh, core), chan(z + ZS - 1, xh, core),
        chan(z, xh, 1 - core), chan(z, 1 - xh, 0), chan(z, 1 - xh, 1),
    ):
        pl.semaphore_signal(barrier, inc=1, device_id=there, device_id_type=MESH)

    def part(hh, cc):
        return pl.ds(pl.multiple_of((hh * 2 + cc) * OWN, OWN), OWN)

    def half(hh):
        return pl.ds(pl.multiple_of(hh * 2 * OWN, 2 * OWN), 2 * OWN)

    def remote(src, dst, s, r, to):
        return pltpu.make_async_remote_copy(
            src_ref=src, dst_ref=dst, send_sem=s, recv_sem=r, device_id=to, device_id_type=MESH
        )

    def up(way, k, cc=None):
        cc = core if cc is None else cc
        return (z + ZS + jnp.where((cc + way) % 2 == 0, k, -k)) % ZS

    loads[0].wait()
    for c in range(ML // 128):
        cols = pl.ds(c * 128, 128)
        send[:, :, cols] = jnp.swapaxes(x_ref[:, :, cols], 0, 1)
    pl.semaphore_wait(barrier, 5)

    def give(p, there, hh, cc):
        q = p // 2
        remote(
            send.at[2 * p + hh], ring.at[q * ZS + there, part(xh, core)], l_send,
            l_recv.at[q, xh * 2 + core], chan(z, hh, cc),
        ).start()

    def got(way, k, hh, cc):
        q = up(way, k) // 2
        block = ring.at[q * ZS + place(way, k), part(hh, cc)]
        remote(block, block, l_send, l_recv.at[q, hh * 2 + cc], chan(z, 1 - xh, core)).wait_recv()

    def z_copy(way, k, j, hh):
        at = (up(way, k) // 2) * ZS + place(way, k + j)
        block = ring.at[at, half(hh)]
        return remote(block, block, z_send, z_recv.at[at, hh], chan(up(way, 1), xh, core))

    def take(way, k, j, hh):
        copy = z_copy(way, k, j, hh)
        copy.wait_recv()
        if k > 0:
            copy.start()

    def take_all(*which):
        for hh in (xh, 1 - xh):
            for way, k, j in which:
                take(way, k, j, hh)

    def rows_of(way, k, lo, n):
        return ring[pl.ds((up(way, k) // 2) * ZS + lo, n)].reshape(n * PER, ML)

    def dot(left, right):
        return lax.dot_general(
            left, right, (((1,), (1,)), ((), ())), preferred_element_type=F32
        ).astype(BF16)

    def weigh(block, p):
        return (block.astype(F32) * w_ref[pl.ds(2 * p + xh, 1), :]).astype(BF16)

    slots = [0]

    def emit(value, p, row_z, lo, n, home=False):
        slot = slots[0]
        slots[0] += 4
        cols = pl.ds(lo * PER, n * PER)
        for i in range(4):
            stage[slot + i, :, 0 : n * PER] = value[i * OWN : (i + 1) * OWN]
        if home:
            found[2 * p + xh, :, cols] = stage[slot + 2 * xh + core, :, 0 : n * PER]
            others = ((xh, 1 - core), (1 - xh, 0), (1 - xh, 1))
        else:
            others = ((0, 0), (0, 1), (1, 0), (1, 1))
        for hh, cc in others:
            remote(
                stage.at[slot + 2 * hh + cc, :, pl.ds(0, n * PER)], found.at[2 * p + xh, :, cols],
                o_send, o_recv, chan(row_z, hh, cc),
            ).start()

    def home(way, k, lo, n):
        p = up(way, k)
        left = weigh(rows_of(way, k, place(way, k), 1), p)
        emit(dot(left, rows_of(way, k, lo, n)), p, z, lo, n, home=True)

    def behind(way, k, j):
        p = up(way, k)
        left = weigh(rows_of(way, k, place(way, k + j), 1), p)
        emit(dot(left, rows_of(way, k, place(way, k), 1)), p, up(way, -j), place(way, k), 1)

    def weigh_all(*places):
        for at in places:
            weighted[at] = weigh(rows_of(0, 0, at, 1), z)

    def across(first, count, lo, n):
        left = weighted[pl.ds(first, count)].reshape(count * PER, ML)
        value = dot(left, rows_of(0, 0, lo, n))
        for i in range(count):
            emit(value[i * PER : (i + 1) * PER], z, up(0, first + i), lo, n)

    def run(e):
        slots[0] = 0
        mine, other = ORDER[e], ORDER[1 - e]
        for (way, k), (oway, ok) in zip(mine, other):
            p, op = up(way, k), up(oway, ok, 1 - core)
            give(op, place(oway, ok), xh, 1 - core)
            give(p, place(way, k), 1 - xh, core)
            give(op, place(oway, ok), 1 - xh, 1 - core)
        for way, k in mine:
            p = up(way, k)
            ring[(p // 2) * ZS + place(way, k), part(xh, core), :] = send[2 * p + xh]
        loads[1].wait()
        weights = w_ref[...]
        w_ref[...] = weights / jnp.sum(weights, axis=1, keepdims=True)

        def side(h):
            return xh if h == 0 else 1 - xh

        def first_half(way, k):
            got(way, k, xh, 1 - core)
            if k > 0:
                z_copy(way, k, 0, xh).start()

        def other_half(way, k):
            got(way, k, 1 - xh, 0)
            got(way, k, 1 - xh, 1)
            if k > 0:
                z_copy(way, k, 0, 1 - xh).start()

        def takes(way, k, j, h):
            take(way, k, j, side(h))

        todo = {
            "F": first_half,
            "O": other_half,
            "T": takes,
            "B": behind,
            "H": home,
            "W": weigh_all,
            "X": across,
        }
        for what, *numbers in PLAN[e]:
            todo[what](*numbers)

        def drain(ref, sem):
            pltpu.make_async_copy(ref, ref, sem).wait()

        drain(stage.at[pl.ds(0, 57 if e == 0 else 59), :, pl.ds(0, 2 * PER)], o_recv)
        for p in range(ZS):
            for place_z in range(ZS):
                at = (place_z - p if p % 2 == 0 else p - place_z) % ZS
                o_ref[2 * p : 2 * p + 2, :, place_z * PER : (place_z + 1) * PER] = found[
                    2 * p : 2 * p + 2, :, at * PER : (at + 1) * PER
                ]
        drain(stage.at[pl.ds(0, 89 if e == 0 else 27), :, pl.ds(0, 2 * PER)], o_send)
        drain(ring.at[pl.ds(0, 6 if e == 0 else 10)], z_send)
        drain(send.at[pl.ds(0, 12)], l_send)

    pl.when((z + core) % 2 == 0)(lambda: run(0))
    pl.when((z + core) % 2 == 1)(lambda: run(1))


def per_device(spectra, weights):
    dma = pltpu.SemaphoreType.DMA
    return pl.pallas_call(
        kernel,
        out_shape=jax.ShapeDtypeStruct((BANDL, OWN, CH), BF16),
        in_specs=[pl.BlockSpec(memory_space=pl.ANY)] * 2,
        out_specs=pl.BlockSpec(memory_space=pltpu.VMEM),
        scratch_shapes=[
            pltpu.VMEM((OWN, BANDL, ML), BF16),
            pltpu.VMEM((BANDL, ML), F32),
            pltpu.VMEM((BANDL, OWN, ML), BF16),
            pltpu.VMEM((4 * ZS, PER, ML), BF16),
            pltpu.VMEM((ZS, PER, ML), BF16),
            pltpu.VMEM((108, OWN, 4 * PER), BF16),
            pltpu.VMEM((BANDL, OWN, CH), BF16),
            dma((2,)),
            dma,
            dma((4, 4)),
            dma,
            dma((4 * ZS, 2)),
            dma,
            dma,
        ],
        compiler_params=pltpu.CompilerParams(
            collective_id=0, has_side_effects=True, vmem_limit_bytes=54000 << 10
        ),
        cost_estimate=pl.CostEstimate(
            flops=2 * BANDL * OWN * CH * ML, bytes_accessed=4 << 20, transcendentals=0
        ),
        name="cross",
    )(spectra, weights)


def solution(mesh):
    placed = (P("chan", "band", None), P("band", None))
    return jax.shard_map(
        per_device, mesh=mesh, in_specs=placed, out_specs=P("band", "chan", None), check_vma=False
    )
```

```python
import jax
import jax.numpy as jnp
from jax import lax
from jax.experimental import pallas as pl
from jax.experimental.pallas import tpu as pltpu
from jax.sharding import PartitionSpec as P

MESH = pl.DeviceIdType.MESH
BF16 = jnp.bfloat16
F32 = jnp.float32

ZS = 8
OWN = 32
PER = 128
BANDL = 16
ML = 1152
CH = 1024

ORDER = (((0, 4), (0, 2), (1, 2), (0, 0)), ((0, 3), (1, 3), (0, 1), (1, 1)))


PLAN = (
    (
        ('F', 0, 4),
        ('F', 1, 2),
        ('F', 0, 2),
        ('F', 0, 0),
        ('O', 0, 4),
        ('T', 1, 2, 1, 0),
        ('T', 0, 2, 1, 0),
        ('O', 0, 2),
        ('O', 1, 2),
        ('T', 1, 2, 1, 1),
        ('T', 0, 2, 1, 1),
        ('B', 0, 2, 1),
        ('B', 1, 2, 1),
        ('O', 0, 0),
        ('T', 0, 2, 2, 0),
        ('T', 0, 2, 2, 1),
        ('T', 0, 0, 1, 0),
        ('T', 0, 0, 1, 1),
        ('T', 1, 0, 1, 0),
        ('T', 1, 0, 1, 1),
        ('W', 0, 7, 1),
        ('X', 7, 1, 0, 2),
        ('X', 1, 1, 0, 1),
        ('B', 0, 2, 2),
        ('T', 0, 0, 2, 0),
        ('T', 0, 0, 2, 1),
        ('T', 1, 0, 2, 0),
        ('T', 1, 0, 2, 1),
        ('W', 6, 2),
        ('X', 6, 1, 0, 3),
        ('X', 2, 1, 0, 1),
        ('X', 1, 2, 6, 2),
        ('T', 0, 0, 3, 0),
        ('T', 0, 0, 3, 1),
        ('T', 1, 0, 3, 0),
        ('T', 1, 0, 3, 1),
        ('W', 5, 3),
        ('X', 5, 1, 0, 4),
        ('X', 7, 1, 2, 2),
        ('X', 3, 1, 6, 2),
        ('X', 6, 1, 3, 1),
        ('X', 3, 1, 0, 1),
        ('H', 0, 4, 4, 1),
        ('H', 0, 2, 4, 3),
        ('H', 1, 2, 2, 2),
        ('T', 0, 0, 4, 0),
        ('T', 0, 0, 4, 1),
        ('W', 4),
        ('X', 4, 1, 0, 4),
        ('X', 1, 3, 4, 2),
        ('H', 0, 0, 0, 4),
        ('H', 0, 0, 4, 4),
    ),
    (
        ('F', 0, 3),
        ('F', 1, 3),
        ('F', 0, 1),
        ('O', 0, 3),
        ('T', 0, 3, 1, 0),
        ('F', 1, 1),
        ('O', 1, 3),
        ('T', 0, 3, 1, 1),
        ('T', 1, 1, 1, 0),
        ('T', 0, 1, 1, 0),
        ('T', 1, 1, 1, 1),
        ('T', 0, 1, 1, 1),
        ('T', 1, 1, 2, 0),
        ('O', 1, 1),
        ('T', 0, 1, 2, 0),
        ('O', 0, 1),
        ('T', 1, 1, 2, 1),
        ('T', 0, 1, 2, 1),
        ('T', 0, 1, 3, 0),
        ('T', 0, 1, 3, 1),
        ('B', 0, 1, 1),
        ('B', 1, 1, 1),
        ('B', 0, 3, 1),
        ('B', 0, 1, 2),
        ('B', 1, 1, 2),
        ('B', 0, 1, 3),
        ('H', 1, 3, 3, 1),
        ('H', 0, 3, 4, 2),
        ('H', 1, 1, 1, 3),
        ('H', 0, 1, 4, 4),
    ),
)


def place(way, k):
    return k if way else (ZS - k) % ZS


def kernel(
    x_hbm, w_hbm, o_ref, x_ref, w_ref, send, ring, weighted, stage, found,
    in_sem, l_send, l_recv, z_send, z_recv, o_send, o_recv,
):
    loads = [
        pltpu.make_async_copy(x_hbm, x_ref, in_sem.at[0]),
        pltpu.make_async_copy(w_hbm, w_ref, in_sem.at[1]),
    ]
    for load in loads:
        load.start()
    dev = lax.axis_index("chan")
    core, xh, z = dev % 2, (dev // 2) % 2, dev // 4

    def chan(zz, xx, cc):
        return {"chan": ((zz % ZS) * 2 + xx) * 2 + cc}

    barrier = pltpu.get_barrier_semaphore()
    for there in (
        chan(z + 1, xh, core), chan(z + ZS - 1, xh, core),
        chan(z, xh, 1 - core), chan(z, 1 - xh, 0), chan(z, 1 - xh, 1),
    ):
        pl.semaphore_signal(barrier, inc=1, device_id=there, device_id_type=MESH)

    def part(hh, cc):
        return pl.ds(pl.multiple_of((hh * 2 + cc) * OWN, OWN), OWN)

    def half(hh):
        return pl.ds(pl.multiple_of(hh * 2 * OWN, 2 * OWN), 2 * OWN)

    def remote(src, dst, s, r, to):
        return pltpu.make_async_remote_copy(
            src_ref=src, dst_ref=dst, send_sem=s, recv_sem=r, device_id=to, device_id_type=MESH
        )

    def up(way, k, cc=None):
        cc = core if cc is None else cc
        return (z + ZS + jnp.where((cc + way) % 2 == 0, k, -k)) % ZS

    loads[0].wait()
    for c in range(ML // 128):
        cols = pl.ds(c * 128, 128)
        send[:, :, cols] = jnp.swapaxes(x_ref[:, :, cols], 0, 1)
    pl.semaphore_wait(barrier, 5)

    def give(p, there, hh, cc):
        q = p // 2
        remote(
            send.at[2 * p + hh], ring.at[q * ZS + there, part(xh, core)], l_send,
            l_recv.at[q, xh * 2 + core], chan(z, hh, cc),
        ).start()

    def got(way, k, hh, cc):
        q = up(way, k) // 2
        block = ring.at[q * ZS + place(way, k), part(hh, cc)]
        remote(block, block, l_send, l_recv.at[q, hh * 2 + cc], chan(z, 1 - xh, core)).wait_recv()

    def z_copy(way, k, j, hh):
        at = (up(way, k) // 2) * ZS + place(way, k + j)
        block = ring.at[at, half(hh)]
        return remote(block, block, z_send, z_recv.at[at, hh], chan(up(way, 1), xh, core))

    def take(way, k, j, hh):
        copy = z_copy(way, k, j, hh)
        copy.wait_recv()
        if k > 0:
            copy.start()

    def take_all(*which):
        for hh in (xh, 1 - xh):
            for way, k, j in which:
                take(way, k, j, hh)

    def rows_of(way, k, lo, n):
        return ring[pl.ds((up(way, k) // 2) * ZS + lo, n)].reshape(n * PER, ML)

    def dot(left, right):
        return lax.dot_general(
            left, right, (((1,), (1,)), ((), ())), preferred_element_type=F32
        ).astype(BF16)

    def weigh(block, p):
        return (block.astype(F32) * w_ref[pl.ds(2 * p + xh, 1), :]).astype(BF16)

    slots = [0]

    def emit(value, p, row_z, lo, n, home=False):
        slot = slots[0]
        slots[0] += 4
        cols = pl.ds(lo * PER, n * PER)
        for i in range(4):
            stage[slot + i, :, 0 : n * PER] = value[i * OWN : (i + 1) * OWN]
        if home:
            found[2 * p + xh, :, cols] = stage[slot + 2 * xh + core, :, 0 : n * PER]
            others = ((xh, 1 - core), (1 - xh, 0), (1 - xh, 1))
        else:
            others = ((0, 0), (0, 1), (1, 0), (1, 1))
        for hh, cc in others:
            remote(
                stage.at[slot + 2 * hh + cc, :, pl.ds(0, n * PER)], found.at[2 * p + xh, :, cols],
                o_send, o_recv, chan(row_z, hh, cc),
            ).start()

    def home(way, k, lo, n):
        p = up(way, k)
        left = weigh(rows_of(way, k, place(way, k), 1), p)
        emit(dot(left, rows_of(way, k, lo, n)), p, z, lo, n, home=True)

    def behind(way, k, j):
        p = up(way, k)
        left = weigh(rows_of(way, k, place(way, k + j), 1), p)
        emit(dot(left, rows_of(way, k, place(way, k), 1)), p, up(way, -j), place(way, k), 1)

    def weigh_all(*places):
        for at in places:
            weighted[at] = weigh(rows_of(0, 0, at, 1), z)

    def across(first, count, lo, n):
        left = weighted[pl.ds(first, count)].reshape(count * PER, ML)
        value = dot(left, rows_of(0, 0, lo, n))
        for i in range(count):
            emit(value[i * PER : (i + 1) * PER], z, up(0, first + i), lo, n)

    def run(e):
        slots[0] = 0
        mine, other = ORDER[e], ORDER[1 - e]
        for (way, k), (oway, ok) in zip(mine, other):
            p, op = up(way, k), up(oway, ok, 1 - core)
            give(op, place(oway, ok), xh, 1 - core)
            give(p, place(way, k), 1 - xh, core)
            give(op, place(oway, ok), 1 - xh, 1 - core)
        for way, k in mine:
            p = up(way, k)
            ring[(p // 2) * ZS + place(way, k), part(xh, core), :] = send[2 * p + xh]
        loads[1].wait()
        weights = w_ref[...]
        w_ref[...] = weights / jnp.sum(weights, axis=1, keepdims=True)

        def side(h):
            return xh if h == 0 else 1 - xh

        def first_half(way, k):
            got(way, k, xh, 1 - core)
            if k > 0:
                z_copy(way, k, 0, xh).start()

        def other_half(way, k):
            got(way, k, 1 - xh, 0)
            got(way, k, 1 - xh, 1)
            if k > 0:
                z_copy(way, k, 0, 1 - xh).start()

        def takes(way, k, j, h):
            take(way, k, j, side(h))

        todo = {
            "F": first_half,
            "O": other_half,
            "T": takes,
            "B": behind,
            "H": home,
            "W": weigh_all,
            "X": across,
        }
        for what, *numbers in PLAN[e]:
            todo[what](*numbers)

        def drain(ref, sem):
            pltpu.make_async_copy(ref, ref, sem).wait()

        drain(stage.at[pl.ds(0, 57 if e == 0 else 59), :, pl.ds(0, 2 * PER)], o_recv)
        for p in range(ZS):
            for place_z in range(ZS):
                at = (place_z - p if p % 2 == 0 else p - place_z) % ZS
                o_ref[2 * p : 2 * p + 2, :, place_z * PER : (place_z + 1) * PER] = found[
                    2 * p : 2 * p + 2, :, at * PER : (at + 1) * PER
                ]
        drain(stage.at[pl.ds(0, 89 if e == 0 else 27), :, pl.ds(0, 2 * PER)], o_send)
        drain(ring.at[pl.ds(0, 6 if e == 0 else 10)], z_send)
        drain(send.at[pl.ds(0, 12)], l_send)

    pl.when((z + core) % 2 == 0)(lambda: run(0))
    pl.when((z + core) % 2 == 1)(lambda: run(1))


def per_device(spectra, weights):
    dma = pltpu.SemaphoreType.DMA
    return pl.pallas_call(
        kernel,
        out_shape=jax.ShapeDtypeStruct((BANDL, OWN, CH), BF16),
        in_specs=[pl.BlockSpec(memory_space=pl.ANY)] * 2,
        out_specs=pl.BlockSpec(memory_space=pltpu.VMEM),
        scratch_shapes=[
            pltpu.VMEM((OWN, BANDL, ML), BF16),
            pltpu.VMEM((BANDL, ML), F32),
            pltpu.VMEM((BANDL, OWN, ML), BF16),
            pltpu.VMEM((4 * ZS, PER, ML), BF16),
            pltpu.VMEM((ZS, PER, ML), BF16),
            pltpu.VMEM((108, OWN, 4 * PER), BF16),
            pltpu.VMEM((BANDL, OWN, CH), BF16),
            dma((2,)),
            dma,
            dma((4, 4)),
            dma,
            dma((4 * ZS, 2)),
            dma,
            dma,
        ],
        compiler_params=pltpu.CompilerParams(
            collective_id=0, has_side_effects=True, vmem_limit_bytes=54000 << 10
        ),
        cost_estimate=pl.CostEstimate(
            flops=2 * BANDL * OWN * CH * ML, bytes_accessed=4 << 20, transcendentals=0
        ),
        name="cross",
    )(spectra, weights)


def solution(mesh):
    placed = (P("chan", "band", None), P("band", None))
    return jax.shard_map(
        per_device, mesh=mesh, in_specs=placed, out_specs=P("band", "chan", None), check_vma=False
    )
```

```python
import jax
import jax.numpy as jnp
from jax import lax
from jax.experimental import pallas as pl
from jax.experimental.pallas import tpu as pltpu
from jax.sharding import PartitionSpec as P

MESH = pl.DeviceIdType.MESH
BF16 = jnp.bfloat16
F32 = jnp.float32

ZS = 8
OWN = 32
PER = 128
BANDL = 16
ML = 1152
CH = 1024

ORDER = (((0, 4), (0, 2), (1, 2), (0, 0)), ((0, 3), (1, 3), (0, 1), (1, 1)))


PLAN = (
    (
        ('F', 0, 4),
        ('F', 0, 2),
        ('F', 1, 2),
        ('F', 0, 0),
        ('O', 0, 4),
        ('T', 0, 2, 1, 0),
        ('T', 1, 2, 1, 0),
        ('O', 0, 2),
        ('O', 1, 2),
        ('T', 0, 2, 1, 1),
        ('T', 1, 2, 1, 1),
        ('O', 0, 0),
        ('T', 0, 2, 2, 0),
        ('T', 0, 2, 2, 1),
        ('B', 0, 2, 1),
        ('B', 1, 2, 1),
        ('B', 0, 2, 2),
        ('T', 0, 0, 1, 0),
        ('T', 0, 0, 1, 1),
        ('T', 1, 0, 1, 0),
        ('T', 1, 0, 1, 1),
        ('W', 3, 4, 5),
        ('X', 3, 1, 4, 2),
        ('X', 5, 1, 3, 2),
        ('T', 0, 0, 2, 0),
        ('T', 0, 0, 2, 1),
        ('T', 1, 0, 2, 0),
        ('T', 1, 0, 2, 1),
        ('W', 2, 6),
        ('X', 2, 1, 4, 3),
        ('X', 6, 1, 2, 3),
        ('T', 1, 0, 3, 0),
        ('T', 1, 0, 3, 1),
        ('W', 7),
        ('X', 7, 1, 2, 3),
        ('X', 3, 1, 6, 2),
        ('X', 2, 1, 7, 1),
        ('T', 0, 0, 3, 0),
        ('T', 0, 0, 3, 1),
        ('W', 1),
        ('X', 1, 1, 4, 4),
        ('H', 0, 4, 0, 1),
        ('H', 0, 2, 0, 3),
        ('H', 1, 2, 6, 2),
        ('T', 0, 0, 4, 0),
        ('T', 0, 0, 4, 1),
        ('W', 0),
        ('X', 0, 1, 4, 4),
        ('X', 6, 2, 0, 2),
        ('X', 5, 1, 0, 3),
        ('H', 0, 0, 4, 4),
        ('H', 0, 0, 0, 4),
    ),
    (
        ('F', 0, 3),
        ('F', 1, 3),
        ('F', 0, 1),
        ('O', 0, 3),
        ('T', 0, 3, 1, 0),
        ('F', 1, 1),
        ('O', 1, 3),
        ('T', 0, 3, 1, 1),
        ('T', 0, 1, 1, 0),
        ('T', 1, 1, 1, 0),
        ('T', 0, 1, 1, 1),
        ('T', 1, 1, 1, 1),
        ('T', 0, 1, 2, 0),
        ('O', 1, 1),
        ('T', 1, 1, 2, 0),
        ('O', 0, 1),
        ('T', 0, 1, 2, 1),
        ('T', 1, 1, 2, 1),
        ('T', 0, 1, 3, 0),
        ('T', 0, 1, 3, 1),
        ('B', 0, 1, 3),
        ('B', 0, 1, 2),
        ('B', 1, 1, 2),
        ('B', 0, 1, 1),
        ('B', 1, 1, 1),
        ('B', 0, 3, 1),
        ('H', 1, 3, 7, 1),
        ('H', 0, 3, 0, 2),
        ('H', 1, 1, 5, 3),
        ('H', 0, 1, 0, 4),
    ),
)


def place(way, k):
    return 4 + k if way else 4 - k


def kernel(
    x_hbm, w_hbm, o_ref, x_ref, w_ref, send, ring, weighted, stage, found,
    in_sem, l_send, l_recv, z_send, z_recv, o_send, o_recv,
):
    loads = [
        pltpu.make_async_copy(x_hbm, x_ref, in_sem.at[0]),
        pltpu.make_async_copy(w_hbm, w_ref, in_sem.at[1]),
    ]
    for load in loads:
        load.start()
    dev = lax.axis_index("chan")
    core, xh, z = dev % 2, (dev // 2) % 2, dev // 4

    def chan(zz, xx, cc):
        return {"chan": ((zz % ZS) * 2 + xx) * 2 + cc}

    barrier = pltpu.get_barrier_semaphore()
    for there in (
        chan(z + 1, xh, core), chan(z + ZS - 1, xh, core),
        chan(z, xh, 1 - core), chan(z, 1 - xh, 0), chan(z, 1 - xh, 1),
    ):
        pl.semaphore_signal(barrier, inc=1, device_id=there, device_id_type=MESH)

    def part(hh, cc):
        return pl.ds(pl.multiple_of((hh * 2 + cc) * OWN, OWN), OWN)

    def half(hh):
        return pl.ds(pl.multiple_of(hh * 2 * OWN, 2 * OWN), 2 * OWN)

    def remote(src, dst, s, r, to):
        return pltpu.make_async_remote_copy(
            src_ref=src, dst_ref=dst, send_sem=s, recv_sem=r, device_id=to, device_id_type=MESH
        )

    def up(way, k, cc=None):
        cc = core if cc is None else cc
        return (z + ZS + jnp.where((cc + way) % 2 == 0, k, -k)) % ZS

    loads[0].wait()
    for c in range(ML // 128):
        cols = pl.ds(c * 128, 128)
        send[:, :, cols] = jnp.swapaxes(x_ref[:, :, cols], 0, 1)
    pl.semaphore_wait(barrier, 5)

    def give(p, there, hh, cc):
        q = p // 2
        remote(
            send.at[2 * p + hh], ring.at[q * ZS + there, part(xh, core)], l_send,
            l_recv.at[q, xh * 2 + core], chan(z, hh, cc),
        ).start()

    def got(way, k, hh, cc):
        q = up(way, k) // 2
        block = ring.at[q * ZS + place(way, k), part(hh, cc)]
        remote(block, block, l_send, l_recv.at[q, hh * 2 + cc], chan(z, 1 - xh, core)).wait_recv()

    def z_copy(way, k, j, hh):
        at = (up(way, k) // 2) * ZS + place(way, k + j)
        block = ring.at[at, half(hh)]
        return remote(block, block, z_send, z_recv.at[at, hh], chan(up(way, 1), xh, core))

    def take(way, k, j, hh):
        copy = z_copy(way, k, j, hh)
        copy.wait_recv()
        if k > 0:
            copy.start()

    def take_all(*which):
        for hh in (xh, 1 - xh):
            for way, k, j in which:
                take(way, k, j, hh)

    def rows_of(way, k, lo, n):
        return ring[pl.ds((up(way, k) // 2) * ZS + lo, n)].reshape(n * PER, ML)

    def dot(left, right):
        return lax.dot_general(
            left, right, (((1,), (1,)), ((), ())), preferred_element_type=F32
        ).astype(BF16)

    def weigh(block, p):
        return (block.astype(F32) * w_ref[pl.ds(2 * p + xh, 1), :]).astype(BF16)

    slots = [0]

    def emit(value, p, row_z, lo, n, home=False):
        slot = slots[0]
        slots[0] += 4
        cols = pl.ds(lo * PER, n * PER)
        for i in range(4):
            stage[slot + i, :, 0 : n * PER] = value[i * OWN : (i + 1) * OWN]
        if home:
            found[2 * p + xh, :, cols] = stage[slot + 2 * xh + core, :, 0 : n * PER]
            others = ((xh, 1 - core), (1 - xh, 0), (1 - xh, 1))
        else:
            others = ((0, 0), (0, 1), (1, 0), (1, 1))
        for hh, cc in others:
            remote(
                stage.at[slot + 2 * hh + cc, :, pl.ds(0, n * PER)], found.at[2 * p + xh, :, cols],
                o_send, o_recv, chan(row_z, hh, cc),
            ).start()

    def home(way, k, lo, n):
        p = up(way, k)
        left = weigh(rows_of(way, k, place(way, k), 1), p)
        emit(dot(left, rows_of(way, k, lo, n)), p, z, lo, n, home=True)

    def behind(way, k, j):
        p = up(way, k)
        left = weigh(rows_of(way, k, place(way, k + j), 1), p)
        emit(dot(left, rows_of(way, k, place(way, k), 1)), p, up(way, -j), place(way, k), 1)

    def weigh_all(*places):
        for at in places:
            weighted[at] = weigh(rows_of(0, 0, at, 1), z)

    def across(first, count, lo, n):
        left = weighted[pl.ds(first, count)].reshape(count * PER, ML)
        value = dot(left, rows_of(0, 0, lo, n))
        for i in range(count):
            emit(value[i * PER : (i + 1) * PER], z, up(0, first + i - 4), lo, n)

    def run(e):
        slots[0] = 0
        mine, other = ORDER[e], ORDER[1 - e]
        for (way, k), (oway, ok) in zip(mine, other):
            p, op = up(way, k), up(oway, ok, 1 - core)
            give(op, place(oway, ok), xh, 1 - core)
            give(p, place(way, k), 1 - xh, core)
            give(op, place(oway, ok), 1 - xh, 1 - core)
        for way, k in mine:
            p = up(way, k)
            ring[(p // 2) * ZS + place(way, k), part(xh, core), :] = send[2 * p + xh]
        loads[1].wait()
        weights = w_ref[...]
        w_ref[...] = weights / jnp.sum(weights, axis=1, keepdims=True)

        def side(h):
            return xh if h == 0 else 1 - xh

        def first_half(way, k):
            got(way, k, xh, 1 - core)
            if k > 0:
                z_copy(way, k, 0, xh).start()

        def other_half(way, k):
            got(way, k, 1 - xh, 0)
            got(way, k, 1 - xh, 1)
            if k > 0:
                z_copy(way, k, 0, 1 - xh).start()

        def takes(way, k, j, h):
            take(way, k, j, side(h))

        todo = {
            "F": first_half,
            "O": other_half,
            "T": takes,
            "B": behind,
            "H": home,
            "W": weigh_all,
            "X": across,
        }
        for what, *numbers in PLAN[e]:
            todo[what](*numbers)

        def drain(ref, sem):
            pltpu.make_async_copy(ref, ref, sem).wait()

        drain(stage.at[pl.ds(0, 57 if e == 0 else 59), :, pl.ds(0, 2 * PER)], o_recv)
        for p in range(ZS):
            for place_z in range(ZS):
                at = (4 + (place_z - p if p % 2 == 0 else p - place_z)) % ZS
                o_ref[2 * p : 2 * p + 2, :, place_z * PER : (place_z + 1) * PER] = found[
                    2 * p : 2 * p + 2, :, at * PER : (at + 1) * PER
                ]
        drain(stage.at[pl.ds(0, 89 if e == 0 else 27), :, pl.ds(0, 2 * PER)], o_send)
        drain(ring.at[pl.ds(0, 6 if e == 0 else 10)], z_send)
        drain(send.at[pl.ds(0, 12)], l_send)

    pl.when((z + core) % 2 == 0)(lambda: run(0))
    pl.when((z + core) % 2 == 1)(lambda: run(1))


def per_device(spectra, weights):
    dma = pltpu.SemaphoreType.DMA
    return pl.pallas_call(
        kernel,
        out_shape=jax.ShapeDtypeStruct((BANDL, OWN, CH), BF16),
        in_specs=[pl.BlockSpec(memory_space=pl.ANY)] * 2,
        out_specs=pl.BlockSpec(memory_space=pltpu.VMEM),
        scratch_shapes=[
            pltpu.VMEM((OWN, BANDL, ML), BF16),
            pltpu.VMEM((BANDL, ML), F32),
            pltpu.VMEM((BANDL, OWN, ML), BF16),
            pltpu.VMEM((4 * ZS, PER, ML), BF16),
            pltpu.VMEM((ZS, PER, ML), BF16),
            pltpu.VMEM((108, OWN, 4 * PER), BF16),
            pltpu.VMEM((BANDL, OWN, CH), BF16),
            dma((2,)),
            dma,
            dma((4, 4)),
            dma,
            dma((4 * ZS, 2)),
            dma,
            dma,
        ],
        compiler_params=pltpu.CompilerParams(
            collective_id=0, has_side_effects=True, vmem_limit_bytes=54000 << 10
        ),
        cost_estimate=pl.CostEstimate(
            flops=2 * BANDL * OWN * CH * ML, bytes_accessed=4 << 20, transcendentals=0
        ),
        name="cross",
    )(spectra, weights)


def solution(mesh):
    placed = (P("chan", "band", None), P("band", None))
    return jax.shard_map(
        per_device, mesh=mesh, in_specs=placed, out_specs=P("band", "chan", None), check_vma=False
    )
```

```python
import jax
import jax.numpy as jnp
from jax import lax
from jax.experimental import pallas as pl
from jax.experimental.pallas import tpu as pltpu
from jax.sharding import PartitionSpec as P

MESH = pl.DeviceIdType.MESH
BF16 = jnp.bfloat16
F32 = jnp.float32

ZS = 8
OWN = 32
PER = 128
BANDL = 16
ML = 1152
CH = 1024

ORDER = (((0, 4), (0, 2), (1, 2), (0, 0)), ((0, 3), (1, 3), (1, 1), (0, 1)))


PLAN = (
    (
        ('F', 0, 4), ('F', 0, 2), ('F', 1, 2), ('F', 0, 0), ('O', 0, 4), ('T', 0, 2, 1, 0), ('T', 1, 2, 1, 0),
        ('O', 0, 2), ('O', 1, 2), ('T', 0, 2, 1, 1), ('T', 1, 2, 1, 1), ('O', 0, 0), ('T', 0, 2, 2, 0),
        ('T', 0, 2, 2, 1), ('B', 0, 2, 2), ('B', 0, 2, 1), ('B', 1, 2, 1), ('T', 0, 0, 1, 0), ('T', 0, 0, 1, 1),
        ('T', 1, 0, 1, 0), ('T', 1, 0, 1, 1), ('W', 3, 4, 5), ('X', 3, 1, 4, 2), ('X', 5, 1, 3, 2), ('T', 0, 0, 2, 0),
        ('T', 0, 0, 2, 1), ('T', 1, 0, 2, 0), ('T', 1, 0, 2, 1), ('W', 2, 6), ('X', 2, 1, 4, 3), ('X', 6, 1, 2, 3),
        ('T', 1, 0, 3, 0), ('T', 1, 0, 3, 1), ('W', 7), ('X', 7, 1, 2, 3), ('X', 3, 1, 6, 2), ('X', 2, 1, 7, 1),
        ('T', 0, 0, 3, 0), ('T', 0, 0, 3, 1), ('W', 1), ('X', 1, 1, 4, 4), ('T', 0, 0, 4, 0), ('T', 0, 0, 4, 1),
        ('W', 0), ('X', 0, 1, 4, 4), ('X', 6, 2, 0, 2), ('X', 5, 1, 0, 3), ('H', 0, 4, 0, 1), ('H', 0, 2, 0, 3),
        ('H', 1, 2, 6, 2), ('H', 0, 0, 4, 4), ('H', 0, 0, 0, 4),
    ),
    (
        ('F', 0, 3), ('F', 1, 3), ('F', 0, 1), ('O', 0, 3), ('T', 0, 3, 1, 0), ('F', 1, 1), ('O', 1, 3),
        ('T', 0, 3, 1, 1), ('T', 0, 1, 1, 0), ('T', 1, 1, 1, 0), ('T', 0, 1, 1, 1), ('T', 1, 1, 1, 1),
        ('T', 0, 1, 2, 0), ('O', 1, 1), ('T', 1, 1, 2, 0), ('O', 0, 1), ('T', 0, 1, 2, 1), ('T', 1, 1, 2, 1),
        ('T', 0, 1, 3, 0), ('T', 0, 1, 3, 1), ('B', 0, 1, 3), ('B', 0, 1, 2), ('B', 1, 1, 2), ('B', 0, 1, 1),
        ('B', 1, 1, 1), ('B', 0, 3, 1), ('H', 1, 3, 7, 1), ('H', 0, 3, 0, 2), ('H', 1, 1, 5, 3), ('H', 0, 1, 0, 4),
    ),
)


def place(way, k):
    return 4 + k if way else 4 - k


def kernel(
    x_hbm, w_hbm, o_ref, x_ref, w_ref, send, ring, weighted, stage, found,
    in_sem, l_send, l_recv, z_send, z_recv, o_send, o_recv,
):
    loads = [
        pltpu.make_async_copy(x_hbm, x_ref, in_sem.at[0]),
        pltpu.make_async_copy(w_hbm, w_ref, in_sem.at[1]),
    ]
    for load in loads:
        load.start()
    dev = lax.axis_index("chan")
    core, xh, z = dev % 2, (dev // 2) % 2, dev // 4

    def chan(zz, xx, cc):
        return {"chan": ((zz % ZS) * 2 + xx) * 2 + cc}

    barrier = pltpu.get_barrier_semaphore()
    for there in (
        chan(z + 1, xh, core), chan(z + ZS - 1, xh, core),
        chan(z, xh, 1 - core), chan(z, 1 - xh, 0), chan(z, 1 - xh, 1),
    ):
        pl.semaphore_signal(barrier, inc=1, device_id=there, device_id_type=MESH)

    def part(hh, cc):
        return pl.ds(pl.multiple_of((hh * 2 + cc) * OWN, OWN), OWN)

    def half(hh):
        return pl.ds(pl.multiple_of(hh * 2 * OWN, 2 * OWN), 2 * OWN)

    def remote(src, dst, s, r, to):
        return pltpu.make_async_remote_copy(
            src_ref=src, dst_ref=dst, send_sem=s, recv_sem=r, device_id=to, device_id_type=MESH
        )

    def up(way, k, cc=None):
        cc = core if cc is None else cc
        return (z + ZS + jnp.where((cc + way) % 2 == 0, k, -k)) % ZS

    loads[0].wait()
    for c in range(ML // 128):
        cols = pl.ds(c * 128, 128)
        send[:, :, cols] = jnp.swapaxes(x_ref[:, :, cols], 0, 1)
    pl.semaphore_wait(barrier, 5)

    def give(p, there, hh, cc):
        q = p // 2
        remote(
            send.at[2 * p + hh], ring.at[q * ZS + there, part(xh, core)], l_send,
            l_recv.at[q, xh * 2 + core], chan(z, hh, cc),
        ).start()

    def got(way, k, hh, cc):
        q = up(way, k) // 2
        block = ring.at[q * ZS + place(way, k), part(hh, cc)]
        remote(block, block, l_send, l_recv.at[q, hh * 2 + cc], chan(z, 1 - xh, core)).wait_recv()

    def z_copy(way, k, j, hh):
        at = (up(way, k) // 2) * ZS + place(way, k + j)
        block = ring.at[at, half(hh)]
        return remote(block, block, z_send, z_recv.at[at, hh], chan(up(way, 1), xh, core))

    def take(way, k, j, hh):
        copy = z_copy(way, k, j, hh)
        copy.wait_recv()
        if k > 0:
            copy.start()

    def take_all(*which):
        for hh in (xh, 1 - xh):
            for way, k, j in which:
                take(way, k, j, hh)

    def rows_of(way, k, lo, n):
        return ring[pl.ds((up(way, k) // 2) * ZS + lo, n)].reshape(n * PER, ML)

    def dot(left, right):
        return lax.dot_general(
            left, right, (((1,), (1,)), ((), ())), preferred_element_type=F32
        ).astype(BF16)

    def weigh(block, p):
        return (block.astype(F32) * w_ref[pl.ds(2 * p + xh, 1), :]).astype(BF16)

    slots = [0]

    def emit(value, p, row_z, lo, n, home=False):
        slot = slots[0]
        slots[0] += 4
        cols = pl.ds(lo * PER, n * PER)
        for i in range(4):
            stage[slot + i, :, 0 : n * PER] = value[i * OWN : (i + 1) * OWN]
        if home:
            found[2 * p + xh, :, cols] = stage[slot + 2 * xh + core, :, 0 : n * PER]
            others = ((xh, 1 - core), (1 - xh, 0), (1 - xh, 1))
        else:
            others = ((0, 0), (0, 1), (1, 0), (1, 1))
        for hh, cc in others:
            remote(
                stage.at[slot + 2 * hh + cc, :, pl.ds(0, n * PER)], found.at[2 * p + xh, :, cols],
                o_send, o_recv, chan(row_z, hh, cc),
            ).start()

    def home(way, k, lo, n):
        p = up(way, k)
        left = weigh(rows_of(way, k, place(way, k), 1), p)
        emit(dot(left, rows_of(way, k, lo, n)), p, z, lo, n, home=True)

    def behind(way, k, j):
        p = up(way, k)
        left = weigh(rows_of(way, k, place(way, k + j), 1), p)
        emit(dot(left, rows_of(way, k, place(way, k), 1)), p, up(way, -j), place(way, k), 1)

    def weigh_all(*places):
        for at in places:
            weighted[at] = weigh(rows_of(0, 0, at, 1), z)

    def across(first, count, lo, n):
        left = weighted[pl.ds(first, count)].reshape(count * PER, ML)
        value = dot(left, rows_of(0, 0, lo, n))
        for i in range(count):
            emit(value[i * PER : (i + 1) * PER], z, up(0, first + i - 4), lo, n)

    def run(e):
        slots[0] = 0
        mine, other = ORDER[e], ORDER[1 - e]
        for (way, k), (oway, ok) in zip(mine, other):
            p, op = up(way, k), up(oway, ok, 1 - core)
            give(op, place(oway, ok), xh, 1 - core)
            give(p, place(way, k), 1 - xh, core)
            give(op, place(oway, ok), 1 - xh, 1 - core)
        for way, k in mine:
            p = up(way, k)
            ring[(p // 2) * ZS + place(way, k), part(xh, core), :] = send[2 * p + xh]
        loads[1].wait()
        weights = w_ref[...]
        w_ref[...] = weights / jnp.sum(weights, axis=1, keepdims=True)

        def side(h):
            return xh if h == 0 else 1 - xh

        def first_half(way, k):
            got(way, k, xh, 1 - core)
            if k > 0:
                z_copy(way, k, 0, xh).start()

        def other_half(way, k):
            got(way, k, 1 - xh, 0)
            got(way, k, 1 - xh, 1)
            if k > 0:
                z_copy(way, k, 0, 1 - xh).start()

        def takes(way, k, j, h):
            take(way, k, j, side(h))

        todo = {
            "F": first_half,
            "O": other_half,
            "T": takes,
            "B": behind,
            "H": home,
            "W": weigh_all,
            "X": across,
        }
        for what, *numbers in PLAN[e]:
            todo[what](*numbers)

        def drain(ref, sem):
            pltpu.make_async_copy(ref, ref, sem).wait()

        drain(stage.at[pl.ds(0, 57 if e == 0 else 59), :, pl.ds(0, 2 * PER)], o_recv)
        for p in range(ZS):
            for place_z in range(ZS):
                at = (4 + (place_z - p if p % 2 == 0 else p - place_z)) % ZS
                o_ref[2 * p : 2 * p + 2, :, place_z * PER : (place_z + 1) * PER] = found[
                    2 * p : 2 * p + 2, :, at * PER : (at + 1) * PER
                ]
        drain(stage.at[pl.ds(0, 89 if e == 0 else 27), :, pl.ds(0, 2 * PER)], o_send)
        drain(ring.at[pl.ds(0, 6 if e == 0 else 10)], z_send)
        drain(send.at[pl.ds(0, 12)], l_send)

    pl.when((z + core) % 2 == 0)(lambda: run(0))
    pl.when((z + core) % 2 == 1)(lambda: run(1))


def per_device(spectra, weights):
    dma = pltpu.SemaphoreType.DMA
    return pl.pallas_call(
        kernel,
        out_shape=jax.ShapeDtypeStruct((BANDL, OWN, CH), BF16),
        in_specs=[pl.BlockSpec(memory_space=pl.ANY)] * 2,
        out_specs=pl.BlockSpec(memory_space=pltpu.VMEM),
        scratch_shapes=[
            pltpu.VMEM((OWN, BANDL, ML), BF16),
            pltpu.VMEM((BANDL, ML), F32),
            pltpu.VMEM((BANDL, OWN, ML), BF16),
            pltpu.VMEM((4 * ZS, PER, ML), BF16),
            pltpu.VMEM((ZS, PER, ML), BF16),
            pltpu.VMEM((108, OWN, 4 * PER), BF16),
            pltpu.VMEM((BANDL, OWN, CH), BF16),
            dma((2,)),
            dma,
            dma((4, 4)),
            dma,
            dma((4 * ZS, 2)),
            dma,
            dma,
        ],
        compiler_params=pltpu.CompilerParams(
            collective_id=0, has_side_effects=True, vmem_limit_bytes=54000 << 10
        ),
        cost_estimate=pl.CostEstimate(
            flops=2 * BANDL * OWN * CH * ML, bytes_accessed=4 << 20, transcendentals=0
        ),
        name="cross",
    )(spectra, weights)


def solution(mesh):
    placed = (P("chan", "band", None), P("band", None))
    return jax.shard_map(
        per_device, mesh=mesh, in_specs=placed, out_specs=P("band", "chan", None), check_vma=False
    )
```

```python
import jax
import jax.numpy as jnp
from jax import lax
from jax.experimental import pallas as pl
from jax.experimental.pallas import tpu as pltpu
from jax.sharding import PartitionSpec as P

MESH = pl.DeviceIdType.MESH
BF16 = jnp.bfloat16
F32 = jnp.float32

ZS = 8
OWN = 32
PER = 128
BANDL = 16
ML = 1152
CH = 1024

ORDER = (((0, 4), (0, 2), (1, 2), (0, 0)), ((0, 3), (1, 3), (1, 1), (0, 1)))


PLAN = (
    (
        ('F', 0, 4), ('F', 0, 2), ('F', 1, 2), ('F', 0, 0), ('O', 0, 4), ('T', 0, 2, 1, 0), ('T', 1, 2, 1, 0),
        ('O', 0, 2), ('O', 1, 2), ('T', 0, 2, 1, 1), ('T', 1, 2, 1, 1), ('O', 0, 0), ('T', 0, 2, 2, 0),
        ('T', 0, 2, 2, 1), ('B', 0, 2, 2), ('B', 0, 2, 1), ('B', 1, 2, 1), ('T', 0, 0, 1, 0), ('T', 0, 0, 1, 1),
        ('T', 1, 0, 1, 0), ('T', 1, 0, 1, 1), ('W', 3, 4, 5), ('X', 3, 1, 4, 2), ('X', 5, 1, 3, 2), ('T', 0, 0, 2, 0),
        ('T', 0, 0, 2, 1), ('T', 1, 0, 2, 0), ('T', 1, 0, 2, 1), ('W', 2, 6), ('X', 2, 1, 4, 3), ('X', 6, 1, 2, 3),
        ('T', 1, 0, 3, 0), ('T', 1, 0, 3, 1), ('W', 7), ('X', 7, 1, 2, 3), ('X', 3, 1, 6, 2), ('X', 2, 1, 7, 1),
        ('T', 0, 0, 3, 0), ('T', 0, 0, 3, 1), ('W', 1), ('X', 1, 1, 4, 4), ('T', 0, 0, 4, 0), ('T', 0, 0, 4, 1),
        ('W', 0), ('X', 0, 1, 4, 2), ('X', 0, 1, 6, 2), ('X', 6, 2, 0, 2), ('X', 5, 1, 0, 3), ('H', 0, 4, 0, 1), ('H', 0, 2, 0, 3),
        ('H', 1, 2, 6, 2), ('H', 0, 0, 4, 4), ('H', 0, 0, 0, 4),
    ),
    (
        ('F', 0, 3), ('F', 1, 3), ('F', 0, 1), ('O', 0, 3), ('T', 0, 3, 1, 0), ('F', 1, 1), ('O', 1, 3),
        ('T', 0, 3, 1, 1), ('T', 0, 1, 1, 0), ('T', 1, 1, 1, 0), ('T', 0, 1, 1, 1), ('T', 1, 1, 1, 1),
        ('T', 0, 1, 2, 0), ('O', 1, 1), ('T', 1, 1, 2, 0), ('O', 0, 1), ('T', 0, 1, 2, 1), ('T', 1, 1, 2, 1),
        ('T', 0, 1, 3, 0), ('T', 0, 1, 3, 1), ('B', 0, 1, 3), ('B', 0, 1, 2), ('B', 1, 1, 2), ('B', 0, 1, 1),
        ('B', 1, 1, 1), ('B', 0, 3, 1), ('H', 1, 3, 7, 1), ('H', 0, 3, 0, 2), ('H', 1, 1, 5, 3), ('H', 0, 1, 0, 4),
    ),
)


def place(way, k):
    return 4 + k if way else 4 - k


def kernel(
    x_hbm, w_hbm, o_ref, x_ref, w_ref, send, ring, weighted, stage, found,
    in_sem, l_send, l_recv, z_send, z_recv, o_send, o_recv,
):
    loads = [
        pltpu.make_async_copy(x_hbm, x_ref, in_sem.at[0]),
        pltpu.make_async_copy(w_hbm, w_ref, in_sem.at[1]),
    ]
    for load in loads:
        load.start()
    dev = lax.axis_index("chan")
    core, xh, z = dev % 2, (dev // 2) % 2, dev // 4

    def chan(zz, xx, cc):
        return {"chan": ((zz % ZS) * 2 + xx) * 2 + cc}

    barrier = pltpu.get_barrier_semaphore()
    for there in (
        chan(z + 1, xh, core), chan(z + ZS - 1, xh, core),
        chan(z, xh, 1 - core), chan(z, 1 - xh, 0), chan(z, 1 - xh, 1),
    ):
        pl.semaphore_signal(barrier, inc=1, device_id=there, device_id_type=MESH)

    def part(hh, cc):
        return pl.ds(pl.multiple_of((hh * 2 + cc) * OWN, OWN), OWN)

    def half(hh):
        return pl.ds(pl.multiple_of(hh * 2 * OWN, 2 * OWN), 2 * OWN)

    def remote(src, dst, s, r, to):
        return pltpu.make_async_remote_copy(
            src_ref=src, dst_ref=dst, send_sem=s, recv_sem=r, device_id=to, device_id_type=MESH
        )

    def up(way, k, cc=None):
        cc = core if cc is None else cc
        return (z + ZS + jnp.where((cc + way) % 2 == 0, k, -k)) % ZS

    loads[0].wait()
    for c in range(ML // 128):
        cols = pl.ds(c * 128, 128)
        send[:, :, cols] = jnp.swapaxes(x_ref[:, :, cols], 0, 1)
    pl.semaphore_wait(barrier, 5)

    def give(p, there, hh, cc):
        q = p // 2
        remote(
            send.at[2 * p + hh], ring.at[q * ZS + there, part(xh, core)], l_send,
            l_recv.at[q, xh * 2 + core], chan(z, hh, cc),
        ).start()

    def got(way, k, hh, cc):
        q = up(way, k) // 2
        block = ring.at[q * ZS + place(way, k), part(hh, cc)]
        remote(block, block, l_send, l_recv.at[q, hh * 2 + cc], chan(z, 1 - xh, core)).wait_recv()

    def z_copy(way, k, j, hh):
        at = (up(way, k) // 2) * ZS + place(way, k + j)
        block = ring.at[at, half(hh)]
        return remote(block, block, z_send, z_recv.at[at, hh], chan(up(way, 1), xh, core))

    def take(way, k, j, hh):
        copy = z_copy(way, k, j, hh)
        copy.wait_recv()
        if k > 0:
            copy.start()

    def take_all(*which):
        for hh in (xh, 1 - xh):
            for way, k, j in which:
                take(way, k, j, hh)

    def rows_of(way, k, lo, n):
        return ring[pl.ds((up(way, k) // 2) * ZS + lo, n)].reshape(n * PER, ML)

    def dot(left, right):
        return lax.dot_general(
            left, right, (((1,), (1,)), ((), ())), preferred_element_type=F32
        ).astype(BF16)

    def weigh(block, p):
        return (block.astype(F32) * w_ref[pl.ds(2 * p + xh, 1), :]).astype(BF16)

    slots = [0]

    def emit(value, p, row_z, lo, n, home=False):
        slot = slots[0]
        slots[0] += 4
        cols = pl.ds(lo * PER, n * PER)
        for i in range(4):
            stage[slot + i, :, 0 : n * PER] = value[i * OWN : (i + 1) * OWN]
        if home:
            found[2 * p + xh, :, cols] = stage[slot + 2 * xh + core, :, 0 : n * PER]
            others = ((xh, 1 - core), (1 - xh, 0), (1 - xh, 1))
        else:
            others = ((0, 0), (0, 1), (1, 0), (1, 1))
        for hh, cc in others:
            remote(
                stage.at[slot + 2 * hh + cc, :, pl.ds(0, n * PER)], found.at[2 * p + xh, :, cols],
                o_send, o_recv, chan(row_z, hh, cc),
            ).start()

    def home(way, k, lo, n):
        p = up(way, k)
        left = weigh(rows_of(way, k, place(way, k), 1), p)
        emit(dot(left, rows_of(way, k, lo, n)), p, z, lo, n, home=True)

    def behind(way, k, j):
        p = up(way, k)
        left = weigh(rows_of(way, k, place(way, k + j), 1), p)
        emit(dot(left, rows_of(way, k, place(way, k), 1)), p, up(way, -j), place(way, k), 1)

    def weigh_all(*places):
        for at in places:
            weighted[at] = weigh(rows_of(0, 0, at, 1), z)

    def across(first, count, lo, n):
        left = weighted[pl.ds(first, count)].reshape(count * PER, ML)
        value = dot(left, rows_of(0, 0, lo, n))
        for i in range(count):
            emit(value[i * PER : (i + 1) * PER], z, up(0, first + i - 4), lo, n)

    def run(e):
        slots[0] = 0
        mine, other = ORDER[e], ORDER[1 - e]
        for (way, k), (oway, ok) in zip(mine, other):
            p, op = up(way, k), up(oway, ok, 1 - core)
            give(op, place(oway, ok), xh, 1 - core)
            give(p, place(way, k), 1 - xh, core)
            give(op, place(oway, ok), 1 - xh, 1 - core)
        for way, k in mine:
            p = up(way, k)
            ring[(p // 2) * ZS + place(way, k), part(xh, core), :] = send[2 * p + xh]
        loads[1].wait()
        weights = w_ref[...]
        w_ref[...] = weights / jnp.sum(weights, axis=1, keepdims=True)

        def side(h):
            return xh if h == 0 else 1 - xh

        def first_half(way, k):
            got(way, k, xh, 1 - core)
            if k > 0:
                z_copy(way, k, 0, xh).start()

        def other_half(way, k):
            got(way, k, 1 - xh, 0)
            got(way, k, 1 - xh, 1)
            if k > 0:
                z_copy(way, k, 0, 1 - xh).start()

        def takes(way, k, j, h):
            take(way, k, j, side(h))

        todo = {
            "F": first_half,
            "O": other_half,
            "T": takes,
            "B": behind,
            "H": home,
            "W": weigh_all,
            "X": across,
        }
        for what, *numbers in PLAN[e]:
            todo[what](*numbers)

        def drain(ref, sem):
            pltpu.make_async_copy(ref, ref, sem).wait()

        drain(stage.at[pl.ds(0, 57 if e == 0 else 59), :, pl.ds(0, 2 * PER)], o_recv)
        for p in range(ZS):
            for place_z in range(ZS):
                at = (4 + (place_z - p if p % 2 == 0 else p - place_z)) % ZS
                o_ref[2 * p : 2 * p + 2, :, place_z * PER : (place_z + 1) * PER] = found[
                    2 * p : 2 * p + 2, :, at * PER : (at + 1) * PER
                ]
        drain(stage.at[pl.ds(0, 89 if e == 0 else 27), :, pl.ds(0, 2 * PER)], o_send)
        drain(ring.at[pl.ds(0, 6 if e == 0 else 10)], z_send)
        drain(send.at[pl.ds(0, 12)], l_send)

    pl.when((z + core) % 2 == 0)(lambda: run(0))
    pl.when((z + core) % 2 == 1)(lambda: run(1))


def per_device(spectra, weights):
    dma = pltpu.SemaphoreType.DMA
    return pl.pallas_call(
        kernel,
        out_shape=jax.ShapeDtypeStruct((BANDL, OWN, CH), BF16),
        in_specs=[pl.BlockSpec(memory_space=pl.ANY)] * 2,
        out_specs=pl.BlockSpec(memory_space=pltpu.VMEM),
        scratch_shapes=[
            pltpu.VMEM((OWN, BANDL, ML), BF16),
            pltpu.VMEM((BANDL, ML), F32),
            pltpu.VMEM((BANDL, OWN, ML), BF16),
            pltpu.VMEM((4 * ZS, PER, ML), BF16),
            pltpu.VMEM((ZS, PER, ML), BF16),
            pltpu.VMEM((108, OWN, 4 * PER), BF16),
            pltpu.VMEM((BANDL, OWN, CH), BF16),
            dma((2,)),
            dma,
            dma((4, 4)),
            dma,
            dma((4 * ZS, 2)),
            dma,
            dma,
        ],
        compiler_params=pltpu.CompilerParams(
            collective_id=0, has_side_effects=True, vmem_limit_bytes=54000 << 10
        ),
        cost_estimate=pl.CostEstimate(
            flops=2 * BANDL * OWN * CH * ML, bytes_accessed=4 << 20, transcendentals=0
        ),
        name="cross",
    )(spectra, weights)


def solution(mesh):
    placed = (P("chan", "band", None), P("band", None))
    return jax.shard_map(
        per_device, mesh=mesh, in_specs=placed, out_specs=P("band", "chan", None), check_vma=False
    )
```
